32 devices in a mesh: tile: 16 (over z, y, core), dir: 2 (over x).
Axes of the slice: x: 2, y: 2, z: 4, core: 2. Of those that a mesh axis runs over, the one named last changes fastest.
Arguments:
- spectrum: float32 [36, 36, 4096], P('dir', None, 'tile'), may hold values from 0.1 to 1
- depths: float32 [4096], P('tile'), may hold values from 2 to 200
- refraction: float32 [2, 4096], P(None, 'tile'), may hold values from -0.22 to 0.22
- edge_geometry: float32 [2, 8, 4096], P(None, None, 'tile'), may hold values from -0.9 to 0.9
- neighbours: int32 [8, 4096], P(None, 'tile'), may hold values from 0 to 287, as said below
- send_rows: int32 [512], P('tile'), may hold values from 0 to 255
- coupling: float32 [36], replicated, may hold values from 0.05 to 0.5
- quad_table: int32 [4, 1296], replicated, may hold values from 0 to 1296, as said below
Outputs:
- spectrum_next: float32 [36, 36, 4096], P('dir', None, 'tile')
The draws below stay inside these ranges and needn't reach their ends.
Inputs may be any that keep to these rules, and one draw needn't show every extreme that they name: `neighbours`: slots of a point beyond its live ones hold the point's own local index and zero edge geometry; index q < 256 is the tile's own point q, 256 + i the i-th point received from the tile below, 272 + i the i-th from the tile above; only points near a tile's edge link to received points. `send_rows`: each tile's block of 32 entries lists first the local points read by the tile below, then those read by the tile above. `quad_table`: 1296 marks a component outside the frequency range; for bin b = j * 36 + i, every component lies in a direction j ± 1 to 4 (mod 36) and a frequency i ± 2 or 3.
All inputs are finite; a program needn't handle non-finite values.
Results may differ from the reference program's by a relative error of at most 0.0003.
Values sent between devices are 32-bit elements; how exact they have to be, the bound alone decides.
A program may use at most 64 MiB of HBM per device.

```python
import math
import jax
import jax.numpy as jnp
from jax import lax

NDIR = 36
NFREQ = 36
NEIGH = 8
PTS_DEV = 256
HALO = 16
NBINS = 1296
POINTS = 4096
SEND = 512
N_TILE = 16


def mesh_links(key):
    live_count = jax.random.randint(jax.random.fold_in(key, 11), (POINTS,), 3, NEIGH + 1)
    slot_index = jnp.arange(NEIGH, dtype=jnp.int32)[:, None]
    is_live = slot_index < live_count[None, :]
    chosen = jax.random.randint(jax.random.fold_in(key, 12), (NEIGH, POINTS), 0, PTS_DEV)
    own_index = jnp.arange(POINTS, dtype=jnp.int32) % PTS_DEV
    lower_edge = own_index < HALO
    upper_edge = own_index >= PTS_DEV - HALO
    remote = jnp.where(lower_edge, PTS_DEV + own_index, PTS_DEV + HALO + own_index - (PTS_DEV - HALO))
    first_slot = jnp.where(lower_edge | upper_edge, remote, chosen[0])
    chosen = chosen.at[0].set(first_slot)
    indices = jnp.where(is_live, chosen, own_index[None, :]).astype(jnp.int32)
    return (indices, is_live)


def draw_neighbours(key, part):
    indices, is_live = mesh_links(key)
    return indices


def draw_edge_geometry(key, part):
    indices, is_live = mesh_links(key)
    raw = jax.random.uniform(jax.random.fold_in(key, 13), (NEIGH, POINTS), jnp.float32, 0.2, 1.0)
    raw = raw * is_live.astype(jnp.float32)
    weights = 0.9 * raw / jnp.sum(raw, axis=0, keepdims=True)
    bearing = jax.random.uniform(jax.random.fold_in(key, 14), (NEIGH, POINTS), jnp.float32, -jnp.pi, jnp.pi)
    return jnp.stack([weights * jnp.cos(bearing), weights * jnp.sin(bearing)], 0).astype(jnp.float32)


def draw_quad_table(key, part):
    off_plus = jax.random.randint(jax.random.fold_in(key, 21), (NFREQ,), 2, 4)
    off_minus = jax.random.randint(jax.random.fold_in(key, 22), (NFREQ,), 2, 4)
    off_minus = off_minus.at[2].set(2)
    turn_small = jax.random.randint(jax.random.fold_in(key, 23), (NFREQ,), 1, 3)
    turn_large = jax.random.randint(jax.random.fold_in(key, 24), (NFREQ,), 3, 5)
    bin_index = jnp.arange(NBINS, dtype=jnp.int32)
    theta_bin = bin_index // NFREQ
    freq_bin = bin_index % NFREQ
    freq_plus = freq_bin + off_plus[freq_bin]
    freq_minus = freq_bin - off_minus[freq_bin]
    plus_valid = freq_plus < NFREQ
    minus_valid = freq_minus >= 0
    small = turn_small[freq_bin]
    large = turn_large[freq_bin]
    plus_one = jnp.where(plus_valid, (theta_bin + small) % NDIR * NFREQ + freq_plus, NBINS)
    minus_one = jnp.where(minus_valid, (theta_bin - large) % NDIR * NFREQ + freq_minus, NBINS)
    plus_two = jnp.where(plus_valid, (theta_bin - small) % NDIR * NFREQ + freq_plus, NBINS)
    minus_two = jnp.where(minus_valid, (theta_bin + large) % NDIR * NFREQ + freq_minus, NBINS)
    return jnp.stack([plus_one, minus_one, plus_two, minus_two], 0).astype(jnp.int32)


def with_ends(entries, rng, low, largest):
    place = [jax.random.randint(jax.random.fold_in(rng, axis), (), 0, length) for axis, length in enumerate(entries.shape)]
    longest = entries.shape.index(max(entries.shape))
    neighbour = place[:longest] + [(place[longest] + 1) % entries.shape[longest]] + place[longest + 1:]
    return entries.at[tuple(place)].set(low).at[tuple(neighbour)].set(largest)


def level_of(own_key, shape, split, least, largest):
    level, own = 1.0, jax.random.fold_in(own_key, 6)
    for axis_at, parts in split:
        heights = jnp.exp(jax.random.uniform(jax.random.fold_in(own, axis_at), (parts,), jnp.float32, least / len(split), largest / len(split)))
        level = level * jnp.repeat(heights, shape[axis_at] // parts).reshape([-1 if axis == axis_at else 1 for axis in range(len(shape))])
    return level


def setup_inputs(seed: int = 0) -> dict:
    key_of = jax.random.split(jax.random.key(seed), 9)
    spectrum = jnp.clip(jnp.exp(math.log(1.0) - 2.3025851 * jax.random.uniform(key_of[0], (NDIR, NFREQ, POINTS), jnp.float32) ** level_of(key_of[0], (NDIR, NFREQ, POINTS), ((0, 2), (2, 16)), -0.2, 0.2)), 0.1, 1.0)
    depths = jnp.clip(jnp.exp(math.log(200.0) - 4.6051702 * jax.random.uniform(key_of[1], (POINTS,), jnp.float32) ** level_of(key_of[1], (POINTS,), ((0, 16),), -0.2, 0.2)), 2.0, 200.0)
    refraction = jnp.clip(jax.random.uniform(key_of[2], (2, POINTS), jnp.float32, -0.22, 0.22) * level_of(key_of[2], (2, POINTS), ((1, 16),), -0.4, 0.0), -0.22, 0.22)
    edge_geometry = draw_edge_geometry(jax.random.fold_in(key_of[8], 71), 0)
    neighbours = draw_neighbours(jax.random.fold_in(key_of[8], 71), 0)
    send_rows = with_ends(jax.random.randint(key_of[5], (SEND,), 0, PTS_DEV), jax.random.fold_in(key_of[5], 1), 0, PTS_DEV - 1).astype(jnp.int32)
    coupling = jnp.clip(jnp.exp(jax.random.uniform(key_of[6], (NFREQ,), jnp.float32, math.log(0.05), math.log(0.5))), 0.05, 0.5)
    quad_table = draw_quad_table(jax.random.fold_in(key_of[8], 71), 0)
    return dict(spectrum=spectrum, depths=depths, refraction=refraction, edge_geometry=edge_geometry, neighbours=neighbours, send_rows=send_rows, coupling=coupling, quad_table=quad_table)


plus_factor = 1.0 / 1.25 ** 4
minus_factor = 1.0 / 0.75 ** 4
cross_factor = 1.0 / 0.9375 ** 4

def wave_speeds(depths, freq_count):
    index = jnp.arange(freq_count, dtype=jnp.int32).astype(jnp.float32)
    ratio = jnp.power(jnp.float32(1.1), index)
    freqs = 0.0418 * ratio
    wavenum = (2.0 * jnp.pi * freqs) ** 2 / 9.81
    shallow = jnp.tanh(wavenum[:, None] * depths[None, :])
    speed = jnp.sqrt(shallow) / ratio[:, None]
    return (speed, 1.0 - shallow)

def angles(dir_index, dir_count):
    return 2.0 * jnp.pi * dir_index.astype(jnp.float32) / dir_count

def turn_rate(turning, refraction, thetas):
    return turning[None] * (jnp.sin(thetas)[:, None, None] * refraction[0][None, None] - jnp.cos(thetas)[:, None, None] * refraction[1][None, None])

def transport(centre, below_dir, above_dir, extended, theta_mid, theta_below, theta_above, depths, refraction, geometry, neighbours):
    speed, turning = wave_speeds(depths, centre.shape[1])
    vel_x = speed[None] * jnp.cos(theta_mid)[:, None, None]
    vel_y = speed[None] * jnp.sin(theta_mid)[:, None, None]
    spatial = jnp.zeros_like(centre)
    for slot_index in range(neighbours.shape[0]):
        flux = vel_x * geometry[0, slot_index] + vel_y * geometry[1, slot_index]
        upwind = jnp.maximum(-flux, 0.0)
        spatial = spatial + upwind * (jnp.take(extended, neighbours[slot_index], axis=2) - centre)
    rate_mid = turn_rate(turning, refraction, theta_mid)
    rate_below = turn_rate(turning, refraction, theta_below)
    rate_above = turn_rate(turning, refraction, theta_above)
    face_above = jnp.maximum(rate_mid, 0.0) * centre + jnp.minimum(rate_above, 0.0) * above_dir
    face_below = jnp.maximum(rate_below, 0.0) * below_dir + jnp.minimum(rate_mid, 0.0) * centre
    return spatial + face_below - face_above

def interactions(spectra, coupling_rows, quad_table):
    bins, columns = spectra.shape
    padded = jnp.concatenate([spectra, jnp.zeros((1, columns), spectra.dtype)], 0)
    source = jnp.zeros((bins + 1, columns), spectra.dtype)
    for config in range(2):
        plus_index = quad_table[2 * config]
        minus_index = quad_table[2 * config + 1]
        plus_vals = padded[plus_index]
        minus_vals = padded[minus_index]
        product = spectra * spectra * (plus_vals * plus_factor + minus_vals * minus_factor) - 2.0 * cross_factor * spectra * plus_vals * minus_vals
        delta = coupling_rows * product
        source = source.at[:bins].add(-2.0 * delta)
        source = source.at[plus_index].add(delta)
        source = source.at[minus_index].add(delta)
    return source[:bins]

def reference(spectrum, depths, refraction, edge_geometry, neighbours, send_rows, coupling, quad_table):
    dir_count, freq_count, total_points = spectrum.shape
    send_table = send_rows.reshape(N_TILE, 2 * HALO)
    coupling_rows = jnp.tile(coupling, dir_count)[:, None]
    dir_index = jnp.arange(dir_count, dtype=jnp.int32)
    theta_mid = angles(dir_index, dir_count)
    theta_below = angles((dir_index - 1) % dir_count, dir_count)
    theta_above = angles((dir_index + 1) % dir_count, dir_count)

    def one_tile(tile_index):
        offset = tile_index * PTS_DEV
        local = lax.dynamic_slice_in_dim(spectrum, offset, PTS_DEV, 2)
        below_tile = jnp.maximum(tile_index - 1, 0)
        above_tile = jnp.minimum(tile_index + 1, N_TILE - 1)
        below_rows = send_table[below_tile, HALO:] + below_tile * PTS_DEV
        above_rows = send_table[above_tile, :HALO] + above_tile * PTS_DEV
        lower_halo = jnp.take(spectrum, below_rows.astype(jnp.int32), axis=2)
        upper_halo = jnp.take(spectrum, above_rows.astype(jnp.int32), axis=2)
        lower_halo = jnp.where(tile_index > 0, lower_halo, jnp.zeros_like(lower_halo))
        upper_halo = jnp.where(tile_index < N_TILE - 1, upper_halo, jnp.zeros_like(upper_halo))
        extended = jnp.concatenate([local, lower_halo, upper_halo], 2)
        tile_depths = lax.dynamic_slice_in_dim(depths, offset, PTS_DEV, 0)
        tile_refraction = lax.dynamic_slice_in_dim(refraction, offset, PTS_DEV, 1)
        tile_geometry = lax.dynamic_slice_in_dim(edge_geometry, offset, PTS_DEV, 2)
        tile_neighbours = lax.dynamic_slice_in_dim(neighbours, offset, PTS_DEV, 1)
        below_dir = jnp.roll(local, 1, axis=0)
        above_dir = jnp.roll(local, -1, axis=0)
        transported = transport(local, below_dir, above_dir, extended, theta_mid, theta_below, theta_above, tile_depths, tile_refraction, tile_geometry, tile_neighbours)
        source = interactions(local.reshape(dir_count * freq_count, PTS_DEV), coupling_rows, quad_table).reshape(dir_count, freq_count, PTS_DEV)
        return local + transported + source
    tiles_out = lax.map(one_tile, jnp.arange(N_TILE, dtype=jnp.int32))
    return jnp.transpose(tiles_out, (1, 2, 0, 3)).reshape(dir_count, freq_count, total_points)
```

```python
import functools
import math

import jax
import jax.numpy as jnp
from jax import lax
from jax.experimental import pallas as pl
from jax.experimental.pallas import tpu as pltpu
from jax.sharding import PartitionSpec as P

plus_factor = 1.0 / 1.25**4
minus_factor = 1.0 / 0.75**4
cross_factor = 1.0 / 0.9375**4
f32, bf16, i32 = jnp.float32, jnp.bfloat16, jnp.int32
REACH = 4
PITCH = 40
PITCH_K = 48
CHUNK = 2
CHUNKS = 4
GROUP = 3


def iota(shape, dim):
    return lax.broadcasted_iota(i32, shape, dim)


def split(x):
    hi = x.astype(bf16)
    lo = (x - hi.astype(f32)).astype(bf16)
    return hi, lo


def one_hot(mask):
    return jnp.where(mask, 1.0, 0.0)


def rows_from(local):
    return lax.reshape(local, (local.shape[0] * local.shape[1], local.shape[2]))


def kernel(
    dirs, freqs, points, halo, slots, tiles,
    spec, dep, refr, geo, nb, srow, coup, table, out,
    e32, ehi, elo, acc, sbuf, rbuf, hsend, hrecv, xcat, spat, wgt, krow, kcol, tab, tabt,
    misc, misci, speed_r, turn_r,
    send_sem, recv_sem, hsend_sem, hrecv_sem,
):
    d = lax.axis_index("dir")
    t = lax.axis_index("tile")
    ndir = 2 * dirs
    bins = ndir * freqs
    first = d * dirs
    own = 2 * REACH
    other = {"dir": 1 - d}

    barrier = pltpu.get_barrier_semaphore()
    pl.semaphore_signal(barrier, inc=1, device_id=other)

    @pl.when(t > 0)
    def _():
        pl.semaphore_signal(barrier, inc=1, device_id={"tile": t - 1})

    @pl.when(t < tiles - 1)
    def _():
        pl.semaphore_signal(barrier, inc=1, device_id={"tile": t + 1})

    def chunk_copy(k):
        return pltpu.make_async_remote_copy(
            src_ref=sbuf.at[k], dst_ref=rbuf.at[k],
            send_sem=send_sem.at[k], recv_sem=recv_sem.at[k],
            device_id=other,
        )

    def chunk_first(k):
        return CHUNK * k if k < CHUNKS else dirs - CHUNK * (k - CHUNKS + 1)

    def chunk_slot(k):
        return own + dirs + CHUNK * k if k < CHUNKS else own - CHUNK * (k - CHUNKS + 1)

    order = [k + half for k in range(CHUNKS) for half in (0, CHUNKS)]
    for k in order:
        for a in range(CHUNK):
            sbuf[k, a * freqs : (a + 1) * freqs, :] = spec[chunk_first(k) + a]
    pl.semaphore_wait(barrier, 1 + (t > 0).astype(i32) + (t < tiles - 1).astype(i32))
    for k in order:
        chunk_copy(k).start()

    zero_tail = jnp.zeros((PITCH_K - PITCH, points), f32)
    e32[...] = jnp.zeros(e32.shape, f32)
    acc[...] = jnp.zeros(acc.shape, f32)

    def keep_split(w):
        hi, lo = split(jnp.concatenate([e32[w], zero_tail], 0))
        ehi[w] = hi
        elo[w] = lo

    for j in range(dirs):
        e32[own + j, 0:freqs, :] = spec[j]
    for j in range(dirs):
        keep_split(own + j)
    own_rows = rows_from(e32[own : own + dirs])
    hi, lo = split(own_rows)
    xcat[:, 0:points] = hi
    xcat[:, points : 2 * points] = lo

    misci[...] = jnp.full(misci.shape, -1, i32)
    misci[0:1, 0 : 2 * halo] = srow[...]
    lane8 = iota((8, 128), 1)
    listed = misci[...]
    down = jnp.where(lane8 < halo, listed, 0)
    up = jnp.where(lane8 < halo, pltpu.roll(listed, 128 - halo, 1), 0)
    for shift in (halo, 2 * halo, 4 * halo):
        down = down + pltpu.roll(down, shift, 1)
        up = up + pltpu.roll(up, shift, 1)
    both = jnp.concatenate([down, up], 1)[0:1]
    sel = one_hot(both == iota((points, 256), 0)).astype(bf16)
    edge = jnp.dot(xcat[:, 0 : 2 * points], jnp.concatenate([sel, sel], 0), preferred_element_type=f32)
    rows_group = GROUP * PITCH
    groups = dirs // GROUP
    lane_group = (iota((rows_group, 256), 1) % 128) // halo
    packed = jnp.zeros((rows_group, 256), f32)
    for r in range(groups):
        packed = jnp.where(lane_group == r, edge[r * rows_group : (r + 1) * rows_group], packed)
    hsend[0] = packed[:, 0:128]
    hsend[1] = packed[:, 128:256]

    def halo_copy(slot, target):
        return pltpu.make_async_remote_copy(
            src_ref=hsend.at[1 - slot], dst_ref=hrecv.at[slot],
            send_sem=hsend_sem.at[slot], recv_sem=hrecv_sem.at[slot],
            device_id={"tile": target},
        )

    @pl.when(t > 0)
    def _():
        halo_copy(1, t - 1).start()

    @pl.when(t < tiles - 1)
    def _():
        halo_copy(0, t + 1).start()

    tab[...] = jnp.full(tab.shape, bins, i32)
    tab[0:4, 0:bins] = table[...]
    raw = tab[...]
    bin_dir = (iota(raw.shape, 1) * 1821) >> 16
    rel = raw - (bin_dir - REACH) * freqs
    rel = jnp.where(rel < 0, rel + bins, rel)
    rel = jnp.where(rel >= bins, rel - bins, rel)
    rel_dir = (rel * 1821) >> 16
    rel_freq = rel - rel_dir * freqs
    rel_slot = jnp.where(rel_dir > REACH, rel_dir - 1, rel_dir)
    missing = raw >= bins
    tab[...] = jnp.where(missing, -1, rel_slot * PITCH + rel_freq)
    in_cols = jnp.where(missing, -1, rel_slot * PITCH_K + rel_freq)
    for b in range(raw.shape[1] // 128):
        block = jnp.concatenate([in_cols[:, 128 * b : 128 * (b + 1)], jnp.zeros((120, 128), i32)], 0)
        tabt[128 * b : 128 * (b + 1), :] = block.T
    kcol[...] = jnp.full(kcol.shape, -1, i32)
    for j in range(ndir):
        start = j * freqs
        kcol[j, 0:freqs, :] = tabt[start : start + freqs, :]
        base = start // 128 * 128
        pair = tab[:, base : base + 256]
        here = pltpu.roll(pair, (256 - (start - base)) % 256, 1)[:, 0:128]
        there = pltpu.roll(here, PITCH, 1)
        rolled = pltpu.roll(there, 8 - 2, 0)
        krow[j] = jnp.where(
            lane8 < freqs, here,
            jnp.where((lane8 >= PITCH) & (lane8 < PITCH + freqs), rolled, -1),
        )
    misc[...] = jnp.zeros(misc.shape, f32)
    misc[0:1, 0:freqs] = coup[...]
    diagonal = iota((PITCH, 128), 0) == iota((PITCH, 128), 1)
    coupling = jnp.sum(jnp.where(diagonal, misc[0:1, :], 0.0), axis=1, keepdims=True)
    coupling = jnp.broadcast_to(coupling, (PITCH, points))

    def quadruplets(w):
        j = lax.rem(first - own + w + ndir, ndir)
        cols = kcol[j]
        lanes = iota((PITCH, 2 * REACH * PITCH_K), 1)
        pick = jnp.concatenate([one_hot(cols[:, c : c + 1] == lanes) for c in range(4)], 0).astype(bf16)
        window = jnp.concatenate(
            [
                rows_from(ref[pl.ds(at, REACH)])
                for ref in (ehi, elo)
                for at in (w - REACH, w + 1)
            ],
            0,
        )
        values = jnp.dot(jnp.concatenate([pick, pick], 1), window, preferred_element_type=f32)
        e = e32[w]
        deltas = []
        for c in range(2):
            plus = values[2 * c * PITCH : (2 * c + 1) * PITCH]
            minus = values[(2 * c + 1) * PITCH : (2 * c + 2) * PITCH]
            deltas.append(
                coupling
                * e
                * (e * (plus * plus_factor + minus * minus_factor) - 2.0 * cross_factor * plus * minus)
            )
        stacked = jnp.concatenate(deltas + [jnp.zeros((128 - 2 * PITCH, points), f32)], 0)
        hi, lo = split(stacked)
        rows = krow[j]
        down_rows = iota((2 * REACH * PITCH, 128), 0)
        place = (one_hot(rows[0:1] == down_rows) + one_hot(rows[1:2] == down_rows)).astype(bf16)
        gained = jnp.dot(
            jnp.concatenate([place, place], 1), jnp.concatenate([hi, lo], 0), preferred_element_type=f32
        )
        gained = gained.reshape(2 * REACH, PITCH, points)
        acc[pl.ds(w - REACH, REACH)] += gained[0:REACH]
        acc[pl.ds(w + 1, REACH)] += gained[REACH : 2 * REACH]
        acc[w] += -2.0 * (deltas[0] + deltas[1])

    def inner(w, carry):
        quadruplets(w)
        return carry

    lax.fori_loop(own + REACH, own + dirs - REACH, inner, 0)

    step = iota((PITCH, points), 0).astype(f32)
    ratio = jnp.exp(step * math.log(1.1))
    wavenum = (2.0 * math.pi * 0.0418 * ratio) ** 2 / 9.81
    shallow = jnp.tanh(wavenum * dep[...])
    speed_r[...] = jnp.sqrt(shallow) / ratio
    turn_r[...] = 1.0 - shallow

    def trig(f, j):
        at = [f(2.0 * math.pi * ((j + s * dirs) % ndir) / ndir) for s in range(2)]
        return jnp.where(d == 0, jnp.float32(at[0]), jnp.float32(at[1]))

    def bend(j):
        return trig(math.sin, j) * refr[0:1] - trig(math.cos, j) * refr[1:2]

    for j in range(dirs):
        flux = trig(math.cos, j) * geo[0] + trig(math.sin, j) * geo[1]
        wgt[j] = jnp.maximum(-flux, 0.0)

    @pl.when(t > 0)
    def _():
        halo_copy(0, t).wait_recv()

    @pl.when(t == 0)
    def _():
        hrecv[0] = jnp.zeros(hrecv.shape[1:], f32)

    @pl.when(t < tiles - 1)
    def _():
        halo_copy(1, t).wait_recv()

    @pl.when(t == tiles - 1)
    def _():
        hrecv[1] = jnp.zeros(hrecv.shape[1:], f32)

    arrived = jnp.concatenate([hrecv[0], hrecv[1]], 1)
    spread = jnp.concatenate([jnp.where(lane_group == r, arrived, 0.0) for r in range(groups)], 0)
    hi, lo = split(spread)
    xcat[:, 2 * points : 2 * points + 256] = hi
    xcat[:, 2 * points + 256 : 2 * points + 512] = lo

    entry = iota((256, points), 0)
    local_ids = iota((points, points), 0)
    halo_ids = points + jnp.where(entry >= 128, halo, 0) + entry % halo
    for s in range(slots):
        who = nb[s : s + 1, :]
        local = one_hot(who == local_ids).astype(bf16)
        edge = one_hot(who == halo_ids).astype(bf16)
        chosen = jnp.dot(
            xcat[...], jnp.concatenate([local, local, edge, edge], 0), preferred_element_type=f32
        ).reshape(dirs, PITCH, points)
        term = wgt[:, s : s + 1, :] * chosen
        if s == 0:
            spat[...] = term
        else:
            spat[...] += term

    for j in range(dirs):
        e = e32[own + j]
        total = jnp.sum(wgt[j], axis=0, keepdims=True)
        turned = -jnp.abs(bend(j)) * e
        if j > 0:
            turned = turned + jnp.maximum(bend(j - 1), 0.0) * e32[own + j - 1]
        if j < dirs - 1:
            turned = turned - jnp.minimum(bend(j + 1), 0.0) * e32[own + j + 1]
        acc[own + j] += e + speed_r[...] * (spat[j] - total * e) + turn_r[...] * turned

    for k in range(CHUNKS):
        for c in (k, CHUNKS + k):
            chunk_copy(c).wait_recv()
            for a in range(CHUNK):
                w = chunk_slot(c) + a
                e32[w, 0:freqs, :] = rbuf[c, a * freqs : (a + 1) * freqs, :]
                keep_split(w)
        if k == 0:
            acc[own] += turn_r[...] * (jnp.maximum(bend(-1), 0.0) * e32[own - 1])
            acc[own + dirs - 1] -= turn_r[...] * (jnp.minimum(bend(dirs), 0.0) * e32[own + dirs])

        def outer(a, carry):
            quadruplets(own + dirs - REACH + CHUNK * k + a)
            quadruplets(own + REACH - 1 - CHUNK * k - a)
            return carry

        lax.fori_loop(0, CHUNK, outer, 0)

    for j in range(dirs):
        out[j] = acc[own + j, 0:freqs, :]

    for k in order:
        chunk_copy(k).wait_send()

    @pl.when(t > 0)
    def _():
        halo_copy(1, t).wait_send()

    @pl.when(t < tiles - 1)
    def _():
        halo_copy(0, t).wait_send()


def body(tiles, spectrum, depths, refraction, edge_geometry, neighbours, send_rows, coupling, quad_table):
    dirs, freqs, points = spectrum.shape
    halo = send_rows.shape[0] // 2
    slots = neighbours.shape[0]
    ndir = 2 * dirs
    window = dirs + 4 * REACH
    lanes = (ndir * freqs + 127) // 128 * 128 + 128
    scratch = [
        pltpu.VMEM((window, PITCH, points), f32),
        pltpu.VMEM((window, PITCH_K, points), bf16),
        pltpu.VMEM((window, PITCH_K, points), bf16),
        pltpu.VMEM((window, PITCH, points), f32),
        pltpu.VMEM((2 * CHUNKS, CHUNK * freqs, points), f32),
        pltpu.VMEM((2 * CHUNKS, CHUNK * freqs, points), f32),
        pltpu.VMEM((2, GROUP * PITCH, 128), f32),
        pltpu.VMEM((2, GROUP * PITCH, 128), f32),
        pltpu.VMEM((dirs * PITCH, 2 * points + 512), bf16),
        pltpu.VMEM((dirs, PITCH, points), f32),
        pltpu.VMEM((dirs, slots, points), f32),
        pltpu.VMEM((ndir, 8, 128), i32),
        pltpu.VMEM((ndir, PITCH, 128), i32),
        pltpu.VMEM((8, lanes), i32),
        pltpu.VMEM((lanes, 128), i32),
        pltpu.VMEM((8, 128), f32),
        pltpu.VMEM((8, 128), i32),
        pltpu.VMEM((PITCH, points), f32),
        pltpu.VMEM((PITCH, points), f32),
        pltpu.SemaphoreType.DMA((2 * CHUNKS,)),
        pltpu.SemaphoreType.DMA((2 * CHUNKS,)),
        pltpu.SemaphoreType.DMA((2,)),
        pltpu.SemaphoreType.DMA((2,)),
    ]
    return pl.pallas_call(
        functools.partial(kernel, dirs, freqs, points, halo, slots, tiles),
        out_shape=jax.ShapeDtypeStruct(spectrum.shape, f32),
        in_specs=[pl.BlockSpec(memory_space=pltpu.VMEM)] * 8,
        out_specs=pl.BlockSpec(memory_space=pltpu.VMEM),
        scratch_shapes=scratch,
        compiler_params=pltpu.CompilerParams(
            collective_id=0, has_side_effects=True, vmem_limit_bytes=40 * 1024 * 1024
        ),
    )(
        spectrum,
        depths.reshape(1, points),
        refraction,
        edge_geometry,
        neighbours,
        send_rows.reshape(1, 2 * halo),
        coupling.reshape(1, freqs),
        quad_table,
    )


def solution(mesh):
    in_specs = (
        P("dir", None, "tile"),
        P("tile"),
        P(None, "tile"),
        P(None, None, "tile"),
        P(None, "tile"),
        P("tile"),
        P(),
        P(),
    )
    out_specs = P("dir", None, "tile")
    return jax.shard_map(
        functools.partial(body, mesh.shape["tile"]),
        mesh=mesh, in_specs=in_specs, out_specs=out_specs, check_vma=False,
    )
```

```python
import functools
import math

import jax
import jax.numpy as jnp
from jax import lax
from jax.experimental import pallas as pl
from jax.experimental.pallas import tpu as pltpu
from jax.sharding import PartitionSpec as P

plus_factor = 1.0 / 1.25**4
minus_factor = 1.0 / 0.75**4
cross_factor = 1.0 / 0.9375**4
f32, bf16, i32 = jnp.float32, jnp.bfloat16, jnp.int32
REACH = 4
PITCH = 40
PITCH_K = 48
CHUNK = 2
CHUNKS = 4
VMEM = 60 * 1024 * 1024
BATCH = 5
GROUP = 3


def iota(shape, dim):
    return lax.broadcasted_iota(i32, shape, dim)


def split(x):
    hi = x.astype(bf16)
    lo = (x - hi.astype(f32)).astype(bf16)
    return hi, lo


def one_hot(mask):
    return jnp.where(mask, 1.0, 0.0)


def rows_from(local):
    return lax.reshape(local, (local.shape[0] * local.shape[1], local.shape[2]))


def kernel(
    dirs, freqs, points, halo, slots, tiles,
    spec, dep_h, refr_h, geo_h, nb_h, srow_h, coup_h, table_h, out,
    e32, dep, refr, geo, nb, srow, coup, table, ehi, elo, acc, sbuf, rbuf, hsend, hrecv, xcat, spat, wgt, krow, kcol, tab, tabt,
    misc, misci, speed_r, turn_r,
    load_sem, send_sem, recv_sem, hsend_sem, hrecv_sem, out_sem,
):
    d = lax.axis_index("dir")
    t = lax.axis_index("tile")
    ndir = 2 * dirs
    bins = ndir * freqs
    first = d * dirs
    own = 2 * REACH
    other = {"dir": 1 - d}

    barrier = pltpu.get_barrier_semaphore()
    pl.semaphore_signal(barrier, inc=1, device_id=other)

    @pl.when(t > 0)
    def _():
        pl.semaphore_signal(barrier, inc=1, device_id={"tile": t - 1})

    @pl.when(t < tiles - 1)
    def _():
        pl.semaphore_signal(barrier, inc=1, device_id={"tile": t + 1})

    def chunk_copy(k):
        return pltpu.make_async_remote_copy(
            src_ref=sbuf.at[k], dst_ref=rbuf.at[k],
            send_sem=send_sem.at[k], recv_sem=recv_sem.at[k],
            device_id=other,
        )

    def chunk_first(k):
        return CHUNK * k if k < CHUNKS else dirs - CHUNK * (k - CHUNKS + 1)

    def chunk_slot(k):
        return own + dirs + CHUNK * k if k < CHUNKS else own - CHUNK * (k - CHUNKS + 1)

    order = [k + half for k in range(CHUNKS) for half in (0, CHUNKS)]
    loads = [pltpu.make_async_copy(spec, e32.at[pl.ds(own, dirs)], load_sem.at[0])]
    for i, (src, dst) in enumerate(
        ((srow_h, srow), (table_h, table), (coup_h, coup), (nb_h, nb), (dep_h, dep), (refr_h, refr), (geo_h, geo))
    ):
        loads.append(pltpu.make_async_copy(src, dst, load_sem.at[i + 1]))
    for load in loads:
        load.start()
    loads[0].wait()
    for k in order:
        for a in range(CHUNK):
            sbuf[k, a * freqs : (a + 1) * freqs, :] = e32[own + chunk_first(k) + a]
    pl.semaphore_wait(barrier, 1 + (t > 0).astype(i32) + (t < tiles - 1).astype(i32))
    for k in order:
        chunk_copy(k).start()

    zero_tail = jnp.zeros((PITCH_K - PITCH, points), f32)
    zero_rows = jnp.zeros((PITCH - freqs, points), f32)
    acc[...] = jnp.zeros(acc.shape, f32)

    def full(w):
        return jnp.concatenate([e32[w], zero_rows], 0)

    def keep_split(w):
        hi, lo = split(jnp.concatenate([full(w), zero_tail], 0))
        ehi[w] = hi
        elo[w] = lo

    for j in range(dirs):
        keep_split(own + j)
    own_rows = jnp.concatenate([full(own + j) for j in range(dirs)], 0)
    hi, lo = split(own_rows)
    xcat[:, 0:points] = hi
    xcat[:, points : 2 * points] = lo

    for load in loads[1:]:
        load.wait()
    misci[...] = jnp.full(misci.shape, -1, i32)
    misci[0:1, 0 : 2 * halo] = srow[...]
    lane8 = iota((8, 128), 1)
    listed = misci[...]
    down = jnp.where(lane8 < halo, listed, 0)
    up = jnp.where(lane8 < halo, pltpu.roll(listed, 128 - halo, 1), 0)
    for shift in (halo, 2 * halo, 4 * halo):
        down = down + pltpu.roll(down, shift, 1)
        up = up + pltpu.roll(up, shift, 1)
    both = jnp.concatenate([down, up], 1)[0:1]
    sel = one_hot(both == iota((points, 256), 0)).astype(bf16)
    edge = jnp.dot(xcat[:, 0 : 2 * points], jnp.concatenate([sel, sel], 0), preferred_element_type=f32)
    rows_group = GROUP * PITCH
    groups = dirs // GROUP
    lane_group = (iota((rows_group, 256), 1) % 128) // halo
    packed = jnp.zeros((rows_group, 256), f32)
    for r in range(groups):
        packed = jnp.where(lane_group == r, edge[r * rows_group : (r + 1) * rows_group], packed)
    hsend[0] = packed[:, 0:128]
    hsend[1] = packed[:, 128:256]

    def halo_copy(slot, target):
        return pltpu.make_async_remote_copy(
            src_ref=hsend.at[1 - slot], dst_ref=hrecv.at[slot],
            send_sem=hsend_sem.at[slot], recv_sem=hrecv_sem.at[slot],
            device_id={"tile": target},
        )

    @pl.when(t > 0)
    def _():
        halo_copy(1, t - 1).start()

    @pl.when(t < tiles - 1)
    def _():
        halo_copy(0, t + 1).start()

    tab[...] = jnp.full(tab.shape, bins, i32)
    tab[0:4, 0:bins] = table[...]
    raw = tab[...]
    bin_dir = (iota(raw.shape, 1) * 1821) >> 16
    rel = raw - (bin_dir - REACH) * freqs
    rel = jnp.where(rel < 0, rel + bins, rel)
    rel = jnp.where(rel >= bins, rel - bins, rel)
    rel_dir = (rel * 1821) >> 16
    rel_freq = rel - rel_dir * freqs
    rel_slot = jnp.where(rel_dir > REACH, rel_dir - 1, rel_dir)
    missing = raw >= bins
    tab[...] = jnp.where(missing, -1, rel_slot * PITCH + rel_freq)
    in_cols = jnp.where(missing, -1, rel_slot * PITCH_K + rel_freq)
    for b in range(raw.shape[1] // 128):
        block = jnp.concatenate([in_cols[:, 128 * b : 128 * (b + 1)], jnp.zeros((120, 128), i32)], 0)
        tabt[128 * b : 128 * (b + 1), :] = block.T
    kcol[...] = jnp.full(kcol.shape, -1, i32)
    for j in range(ndir):
        start = j * freqs
        kcol[j, 0:freqs, :] = tabt[start : start + freqs, :]
        base = start // 128 * 128
        pair = tab[:, base : base + 256]
        here = pltpu.roll(pair, (256 - (start - base)) % 256, 1)[:, 0:128]
        there = pltpu.roll(here, PITCH, 1)
        rolled = pltpu.roll(there, 8 - 2, 0)
        krow[j] = jnp.where(
            lane8 < freqs, here,
            jnp.where((lane8 >= PITCH) & (lane8 < PITCH + freqs), rolled, -1),
        )
    misc[...] = jnp.zeros(misc.shape, f32)
    misc[0:1, 0:freqs] = coup[...]
    diagonal = iota((PITCH, 128), 0) == iota((PITCH, 128), 1)
    coupling = jnp.sum(jnp.where(diagonal, misc[0:1, :], 0.0), axis=1, keepdims=True)
    coupling = jnp.broadcast_to(coupling, (PITCH, points))

    pick_lanes = iota((PITCH, 2 * REACH * PITCH_K), 1)
    place_rows = iota((2 * REACH * PITCH, 128), 0)

    def gathered(w, j):
        cols = kcol[j]
        pick = jnp.concatenate([one_hot(cols[:, c : c + 1] == pick_lanes) for c in range(4)], 0).astype(bf16)
        window = jnp.concatenate(
            [rows_from(ref[pl.ds(at, REACH)]) for ref in (ehi, elo) for at in (w - REACH, w + 1)], 0
        )
        return jnp.dot(jnp.concatenate([pick, pick], 1), window, preferred_element_type=f32)

    def exchanged(w, values):
        e = full(w)
        deltas = []
        for c in range(2):
            plus = values[2 * c * PITCH : (2 * c + 1) * PITCH]
            minus = values[(2 * c + 1) * PITCH : (2 * c + 2) * PITCH]
            deltas.append(
                coupling
                * e
                * (e * (plus * plus_factor + minus * minus_factor) - 2.0 * cross_factor * plus * minus)
            )
        return deltas

    def scattered(w, j, deltas):
        stacked = jnp.concatenate(deltas + [jnp.zeros((128 - 2 * PITCH, points), f32)], 0)
        hi, lo = split(stacked)
        rows = krow[j]
        place = (one_hot(rows[0:1] == place_rows) + one_hot(rows[1:2] == place_rows)).astype(bf16)
        gained = jnp.dot(
            jnp.concatenate([place, place], 1), jnp.concatenate([hi, lo], 0), preferred_element_type=f32
        )
        return gained.reshape(2 * REACH, PITCH, points)

    def quadruplets(slots_at):
        js = [lax.rem(first - own + w + ndir, ndir) for w in slots_at]
        values = [gathered(w, j) for w, j in zip(slots_at, js)]
        deltas = [exchanged(w, v) for w, v in zip(slots_at, values)]
        gains = [scattered(w, j, x) for w, j, x in zip(slots_at, js, deltas)]
        for w, x, gained in zip(slots_at, deltas, gains):
            acc[pl.ds(w - REACH, REACH)] += gained[0:REACH, 0:freqs]
            acc[pl.ds(w + 1, REACH)] += gained[REACH : 2 * REACH, 0:freqs]
            acc[w] += (-2.0 * (x[0] + x[1]))[0:freqs]

    def inner(a, carry):
        quadruplets([own + REACH + a * BATCH + b for b in range(BATCH)])
        return carry

    lax.fori_loop(0, (dirs - 2 * REACH) // BATCH, inner, 0)

    step = iota((PITCH, points), 0).astype(f32)
    ratio = jnp.exp(step * math.log(1.1))
    wavenum = (2.0 * math.pi * 0.0418 * ratio) ** 2 / 9.81
    shallow = jnp.tanh(wavenum * dep[...])
    speed_r[...] = jnp.sqrt(shallow) / ratio
    turn_r[...] = 1.0 - shallow

    def trig(f, j):
        at = [f(2.0 * math.pi * ((j + s * dirs) % ndir) / ndir) for s in range(2)]
        return jnp.where(d == 0, jnp.float32(at[0]), jnp.float32(at[1]))

    def bend(j):
        return trig(math.sin, j) * refr[0:1] - trig(math.cos, j) * refr[1:2]

    for j in range(dirs):
        flux = trig(math.cos, j) * geo[0] + trig(math.sin, j) * geo[1]
        wgt[j] = jnp.maximum(-flux, 0.0)

    @pl.when(t > 0)
    def _():
        halo_copy(0, t).wait_recv()

    @pl.when(t == 0)
    def _():
        hrecv[0] = jnp.zeros(hrecv.shape[1:], f32)

    @pl.when(t < tiles - 1)
    def _():
        halo_copy(1, t).wait_recv()

    @pl.when(t == tiles - 1)
    def _():
        hrecv[1] = jnp.zeros(hrecv.shape[1:], f32)

    arrived = jnp.concatenate([hrecv[0], hrecv[1]], 1)
    spread = jnp.concatenate([jnp.where(lane_group == r, arrived, 0.0) for r in range(groups)], 0)
    hi, lo = split(spread)
    xcat[:, 2 * points : 2 * points + 256] = hi
    xcat[:, 2 * points + 256 : 2 * points + 512] = lo

    entry = iota((256, points), 0)
    local_ids = iota((points, points), 0)
    halo_ids = points + jnp.where(entry >= 128, halo, 0) + entry % halo
    for s in range(slots):
        who = nb[s : s + 1, :]
        local = one_hot(who == local_ids).astype(bf16)
        edge = one_hot(who == halo_ids).astype(bf16)
        chosen = jnp.dot(
            xcat[...], jnp.concatenate([local, local, edge, edge], 0), preferred_element_type=f32
        ).reshape(dirs, PITCH, points)
        term = wgt[:, s : s + 1, :] * chosen
        if s == 0:
            spat[...] = term
        else:
            spat[...] += term

    for j in range(dirs):
        e = full(own + j)
        total = jnp.sum(wgt[j], axis=0, keepdims=True)
        turned = -jnp.abs(bend(j)) * e
        if j > 0:
            turned = turned + jnp.maximum(bend(j - 1), 0.0) * full(own + j - 1)
        if j < dirs - 1:
            turned = turned - jnp.minimum(bend(j + 1), 0.0) * full(own + j + 1)
        acc[own + j] += (e + speed_r[...] * (spat[j] - total * e) + turn_r[...] * turned)[0:freqs]

    stores = []
    for k in range(CHUNKS):
        for c in (k, CHUNKS + k):
            chunk_copy(c).wait_recv()
            for a in range(CHUNK):
                w = chunk_slot(c) + a
                e32[w] = rbuf[c, a * freqs : (a + 1) * freqs, :]
                keep_split(w)
        if k == 0:
            acc[own] += turn_r[0:freqs] * (jnp.maximum(bend(-1), 0.0) * e32[own - 1])
            acc[own + dirs - 1] -= turn_r[0:freqs] * (jnp.minimum(bend(dirs), 0.0) * e32[own + dirs])

        quadruplets(
            [own + dirs - REACH + CHUNK * k + a for a in range(CHUNK)]
            + [own + REACH - 1 - CHUNK * k - a for a in range(CHUNK)]
        )
        low, high = 2 * REACH - 2 - CHUNK * k, dirs - 2 * REACH + 2 + CHUNK * k
        parts = [(low, high)] if k == 0 else [(low, low + CHUNK), (high - CHUNK, high)]
        for lo_dir, hi_dir in parts:
            store = pltpu.make_async_copy(
                acc.at[pl.ds(own + lo_dir, hi_dir - lo_dir)],
                out.at[pl.ds(lo_dir, hi_dir - lo_dir)],
                out_sem.at[len(stores)],
            )
            store.start()
            stores.append(store)

    for store in stores:
        store.wait()
    for k in order:
        chunk_copy(k).wait_send()

    @pl.when(t > 0)
    def _():
        halo_copy(1, t).wait_send()

    @pl.when(t < tiles - 1)
    def _():
        halo_copy(0, t).wait_send()


def body(tiles, spectrum, depths, refraction, edge_geometry, neighbours, send_rows, coupling, quad_table):
    dirs, freqs, points = spectrum.shape
    halo = send_rows.shape[0] // 2
    slots = neighbours.shape[0]
    ndir = 2 * dirs
    window = dirs + 4 * REACH
    lanes = (ndir * freqs + 127) // 128 * 128 + 128
    scratch = [
        pltpu.VMEM((window, freqs, points), f32),
        pltpu.VMEM((1, points), f32),
        pltpu.VMEM(refraction.shape, f32),
        pltpu.VMEM(edge_geometry.shape, f32),
        pltpu.VMEM(neighbours.shape, i32),
        pltpu.VMEM((1, 2 * halo), i32),
        pltpu.VMEM((1, freqs), f32),
        pltpu.VMEM(quad_table.shape, i32),
        pltpu.VMEM((window, PITCH_K, points), bf16),
        pltpu.VMEM((window, PITCH_K, points), bf16),
        pltpu.VMEM((window, freqs, points), f32),
        pltpu.VMEM((2 * CHUNKS, CHUNK * freqs, points), f32),
        pltpu.VMEM((2 * CHUNKS, CHUNK * freqs, points), f32),
        pltpu.VMEM((2, GROUP * PITCH, 128), f32),
        pltpu.VMEM((2, GROUP * PITCH, 128), f32),
        pltpu.VMEM((dirs * PITCH, 2 * points + 512), bf16),
        pltpu.VMEM((dirs, PITCH, points), f32),
        pltpu.VMEM((dirs, slots, points), f32),
        pltpu.VMEM((ndir, 8, 128), i32),
        pltpu.VMEM((ndir, PITCH, 128), i32),
        pltpu.VMEM((8, lanes), i32),
        pltpu.VMEM((lanes, 128), i32),
        pltpu.VMEM((8, 128), f32),
        pltpu.VMEM((8, 128), i32),
        pltpu.VMEM((PITCH, points), f32),
        pltpu.VMEM((PITCH, points), f32),
        pltpu.SemaphoreType.DMA((8,)),
        pltpu.SemaphoreType.DMA((2 * CHUNKS,)),
        pltpu.SemaphoreType.DMA((2 * CHUNKS,)),
        pltpu.SemaphoreType.DMA((2,)),
        pltpu.SemaphoreType.DMA((2,)),
        pltpu.SemaphoreType.DMA((2 * CHUNKS - 1,)),
    ]
    return pl.pallas_call(
        functools.partial(kernel, dirs, freqs, points, halo, slots, tiles),
        out_shape=jax.ShapeDtypeStruct(spectrum.shape, f32),
        in_specs=[pl.BlockSpec(memory_space=pl.ANY)] * 8,
        out_specs=pl.BlockSpec(memory_space=pl.ANY),
        scratch_shapes=scratch,
        compiler_params=pltpu.CompilerParams(
            collective_id=0, has_side_effects=True, vmem_limit_bytes=VMEM
        ),
    )(
        spectrum,
        depths.reshape(1, points),
        refraction,
        edge_geometry,
        neighbours,
        send_rows.reshape(1, 2 * halo),
        coupling.reshape(1, freqs),
        quad_table,
    )


def solution(mesh):
    in_specs = (
        P("dir", None, "tile"),
        P("tile"),
        P(None, "tile"),
        P(None, None, "tile"),
        P(None, "tile"),
        P("tile"),
        P(),
        P(),
    )
    out_specs = P("dir", None, "tile")
    return jax.shard_map(
        functools.partial(body, mesh.shape["tile"]),
        mesh=mesh, in_specs=in_specs, out_specs=out_specs, check_vma=False,
    )
```

```python
import functools
import math

import jax
import jax.numpy as jnp
from jax import lax
from jax.experimental import pallas as pl
from jax.experimental.pallas import tpu as pltpu
from jax.sharding import PartitionSpec as P

plus_factor = 1.0 / 1.25**4
minus_factor = 1.0 / 0.75**4
cross_factor = 1.0 / 0.9375**4
f32, bf16, i32 = jnp.float32, jnp.bfloat16, jnp.int32
REACH = 4
PITCH = 40
PITCH_K = 48
CHUNK = 2
CHUNKS = 4
VMEM = 61440 * 1024
BATCH = 5
GROUP = 3


def iota(shape, dim):
    return lax.broadcasted_iota(i32, shape, dim)


def split(x):
    hi = x.astype(bf16)
    lo = (x - hi.astype(f32)).astype(bf16)
    return hi, lo


def one_hot(mask):
    return jnp.where(mask, 1.0, 0.0)


def rows_from(local):
    return lax.reshape(local, (local.shape[0] * local.shape[1], local.shape[2]))


def kernel(
    dirs, freqs, points, halo, slots, tiles,
    spec, dep_h, refr_h, geo_h, nb_h, srow_h, coup_h, table_h, out,
    e32, dep, refr, geo, nb, srow, coup, table, ehi, elo, acc, sbuf, rbuf, hsend, hrecv, xcat, spat, wgt, krow, kcol, tab, tabt,
    misc, misci, speed_r, turn_r,
    load_sem, send_sem, recv_sem, hsend_sem, hrecv_sem,
):
    d = lax.axis_index("dir")
    t = lax.axis_index("tile")
    ndir = 2 * dirs
    bins = ndir * freqs
    first = d * dirs
    own = 2 * REACH
    other = {"dir": 1 - d}

    barrier = pltpu.get_barrier_semaphore()
    pl.semaphore_signal(barrier, inc=1, device_id=other)

    @pl.when(t > 0)
    def _():
        pl.semaphore_signal(barrier, inc=1, device_id={"tile": t - 1})

    @pl.when(t < tiles - 1)
    def _():
        pl.semaphore_signal(barrier, inc=1, device_id={"tile": t + 1})

    def chunk_copy(k):
        return pltpu.make_async_remote_copy(
            src_ref=sbuf.at[k], dst_ref=rbuf.at[k],
            send_sem=send_sem.at[k], recv_sem=recv_sem.at[k],
            device_id=other,
        )

    def chunk_first(k):
        return CHUNK * k if k < CHUNKS else dirs - CHUNK * (k - CHUNKS + 1)

    def chunk_slot(k):
        return own + dirs + CHUNK * k if k < CHUNKS else own - CHUNK * (k - CHUNKS + 1)

    order = [k + half for k in range(CHUNKS) for half in (0, CHUNKS)]
    def spec_load(at, count, sem):
        return pltpu.make_async_copy(spec.at[pl.ds(at, count)], e32.at[pl.ds(own + at, count)], load_sem.at[sem])

    middle = CHUNK * CHUNKS
    spec_loads = [spec_load(chunk_first(k), CHUNK, i) for i, k in enumerate(order)]
    spec_loads.append(spec_load(middle, dirs - 2 * middle, len(order)))
    loads = []
    for i, (src, dst) in enumerate(
        ((srow_h, srow), (table_h, table), (coup_h, coup), (nb_h, nb), (dep_h, dep), (refr_h, refr), (geo_h, geo))
    ):
        loads.append(pltpu.make_async_copy(src, dst, load_sem.at[len(order) + 1 + i]))
    for load in spec_loads + loads:
        load.start()
    for i, k in enumerate(order):
        spec_loads[i].wait()
        for a in range(CHUNK):
            sbuf[k, a * freqs : (a + 1) * freqs, :] = e32[own + chunk_first(k) + a]
        if i == 0:
            pl.semaphore_wait(barrier, 1 + (t > 0).astype(i32) + (t < tiles - 1).astype(i32))
        chunk_copy(k).start()
    spec_loads[-1].wait()

    zero_tail = jnp.zeros((PITCH_K - PITCH, points), f32)
    zero_rows = jnp.zeros((PITCH - freqs, points), f32)
    acc[...] = jnp.zeros(acc.shape, f32)

    def full(w):
        return jnp.concatenate([e32[w], zero_rows], 0)

    def keep_split(w):
        hi, lo = split(jnp.concatenate([full(w), zero_tail], 0))
        ehi[w] = hi
        elo[w] = lo

    for j in range(dirs):
        keep_split(own + j)
    own_rows = jnp.concatenate([full(own + j) for j in range(dirs)], 0)
    hi, lo = split(own_rows)
    xcat[:, 0:points] = hi
    xcat[:, points : 2 * points] = lo

    for load in loads:
        load.wait()
    misci[...] = jnp.full(misci.shape, -1, i32)
    misci[0:1, 0 : 2 * halo] = srow[...]
    lane8 = iota((8, 128), 1)
    listed = misci[...]
    down = jnp.where(lane8 < halo, listed, 0)
    up = jnp.where(lane8 < halo, pltpu.roll(listed, 128 - halo, 1), 0)
    for shift in (halo, 2 * halo, 4 * halo):
        down = down + pltpu.roll(down, shift, 1)
        up = up + pltpu.roll(up, shift, 1)
    both = jnp.concatenate([down, up], 1)[0:1]
    sel = one_hot(both == iota((points, 256), 0)).astype(bf16)
    edge = jnp.dot(xcat[:, 0 : 2 * points], jnp.concatenate([sel, sel], 0), preferred_element_type=f32)
    rows_group = GROUP * PITCH
    groups = dirs // GROUP
    lane_group = (iota((rows_group, 256), 1) % 128) // halo
    packed = jnp.zeros((rows_group, 256), f32)
    for r in range(groups):
        packed = jnp.where(lane_group == r, edge[r * rows_group : (r + 1) * rows_group], packed)
    hsend[0] = packed[:, 0:128]
    hsend[1] = packed[:, 128:256]

    def halo_copy(slot, target):
        return pltpu.make_async_remote_copy(
            src_ref=hsend.at[1 - slot], dst_ref=hrecv.at[slot],
            send_sem=hsend_sem.at[slot], recv_sem=hrecv_sem.at[slot],
            device_id={"tile": target},
        )

    @pl.when(t > 0)
    def _():
        halo_copy(1, t - 1).start()

    @pl.when(t < tiles - 1)
    def _():
        halo_copy(0, t + 1).start()

    tab[...] = jnp.full(tab.shape, bins, i32)
    tab[0:4, 0:bins] = table[...]
    raw = tab[...]
    bin_dir = (iota(raw.shape, 1) * 1821) >> 16
    rel = raw - (bin_dir - REACH) * freqs
    rel = jnp.where(rel < 0, rel + bins, rel)
    rel = jnp.where(rel >= bins, rel - bins, rel)
    rel_dir = (rel * 1821) >> 16
    rel_freq = rel - rel_dir * freqs
    rel_slot = jnp.where(rel_dir > REACH, rel_dir - 1, rel_dir)
    missing = raw >= bins
    tab[...] = jnp.where(missing, -1, rel_slot * PITCH + rel_freq)
    in_cols = jnp.where(missing, -1, rel_slot * PITCH_K + rel_freq)
    for b in range(raw.shape[1] // 128):
        block = jnp.concatenate([in_cols[:, 128 * b : 128 * (b + 1)], jnp.zeros((120, 128), i32)], 0)
        tabt[128 * b : 128 * (b + 1), :] = block.T
    kcol[...] = jnp.full(kcol.shape, -1, i32)
    for j in range(ndir):
        start = j * freqs
        kcol[j, 0:freqs, :] = tabt[start : start + freqs, :]
        base = start // 128 * 128
        pair = tab[:, base : base + 256]
        here = pltpu.roll(pair, (256 - (start - base)) % 256, 1)[:, 0:128]
        there = pltpu.roll(here, PITCH, 1)
        rolled = pltpu.roll(there, 8 - 2, 0)
        krow[j] = jnp.where(
            lane8 < freqs, here,
            jnp.where((lane8 >= PITCH) & (lane8 < PITCH + freqs), rolled, -1),
        )
    misc[...] = jnp.zeros(misc.shape, f32)
    misc[0:1, 0:freqs] = coup[...]
    diagonal = iota((PITCH, 128), 0) == iota((PITCH, 128), 1)
    coupling = jnp.sum(jnp.where(diagonal, misc[0:1, :], 0.0), axis=1, keepdims=True)
    coupling = jnp.broadcast_to(coupling, (PITCH, points))

    pick_lanes = iota((PITCH, 2 * REACH * PITCH_K), 1)
    place_rows = iota((2 * REACH * PITCH, 128), 0)

    def gathered(w, j):
        cols = kcol[j]
        pick = jnp.concatenate([one_hot(cols[:, c : c + 1] == pick_lanes) for c in range(4)], 0).astype(bf16)
        window = jnp.concatenate(
            [rows_from(ref[pl.ds(at, REACH)]) for ref in (ehi, elo) for at in (w - REACH, w + 1)], 0
        )
        return jnp.dot(jnp.concatenate([pick, pick], 1), window, preferred_element_type=f32)

    def exchanged(w, values):
        e = full(w)
        deltas = []
        for c in range(2):
            plus = values[2 * c * PITCH : (2 * c + 1) * PITCH]
            minus = values[(2 * c + 1) * PITCH : (2 * c + 2) * PITCH]
            deltas.append(
                coupling
                * e
                * (e * (plus * plus_factor + minus * minus_factor) - 2.0 * cross_factor * plus * minus)
            )
        return deltas

    def scattered(w, j, deltas):
        stacked = jnp.concatenate(deltas + [jnp.zeros((128 - 2 * PITCH, points), f32)], 0)
        hi, lo = split(stacked)
        rows = krow[j]
        place = (one_hot(rows[0:1] == place_rows) + one_hot(rows[1:2] == place_rows)).astype(bf16)
        gained = jnp.dot(
            jnp.concatenate([place, place], 1), jnp.concatenate([hi, lo], 0), preferred_element_type=f32
        )
        return gained.reshape(2 * REACH, PITCH, points)

    def quadruplets(slots_at):
        js = [lax.rem(first - own + w + ndir, ndir) for w in slots_at]
        values = [gathered(w, j) for w, j in zip(slots_at, js)]
        deltas = [exchanged(w, v) for w, v in zip(slots_at, values)]
        gains = [scattered(w, j, x) for w, j, x in zip(slots_at, js, deltas)]
        for w, x, gained in zip(slots_at, deltas, gains):
            acc[pl.ds(w - REACH, REACH)] += gained[0:REACH, 0:freqs]
            acc[pl.ds(w + 1, REACH)] += gained[REACH : 2 * REACH, 0:freqs]
            acc[w] += (-2.0 * (x[0] + x[1]))[0:freqs]

    def inner(a, carry):
        quadruplets([own + REACH + a * BATCH + b for b in range(BATCH)])
        return carry

    lax.fori_loop(0, (dirs - 2 * REACH) // BATCH, inner, 0)

    step = iota((PITCH, points), 0).astype(f32)
    ratio = jnp.exp(step * math.log(1.1))
    wavenum = (2.0 * math.pi * 0.0418 * ratio) ** 2 / 9.81
    shallow = jnp.tanh(wavenum * dep[...])
    speed_r[...] = jnp.sqrt(shallow) / ratio
    turn_r[...] = 1.0 - shallow

    def trig(f, j):
        at = [f(2.0 * math.pi * ((j + s * dirs) % ndir) / ndir) for s in range(2)]
        return jnp.where(d == 0, jnp.float32(at[0]), jnp.float32(at[1]))

    def bend(j):
        return trig(math.sin, j) * refr[0:1] - trig(math.cos, j) * refr[1:2]

    for j in range(dirs):
        flux = trig(math.cos, j) * geo[0] + trig(math.sin, j) * geo[1]
        wgt[j] = jnp.maximum(-flux, 0.0)

    @pl.when(t > 0)
    def _():
        halo_copy(0, t).wait_recv()

    @pl.when(t == 0)
    def _():
        hrecv[0] = jnp.zeros(hrecv.shape[1:], f32)

    @pl.when(t < tiles - 1)
    def _():
        halo_copy(1, t).wait_recv()

    @pl.when(t == tiles - 1)
    def _():
        hrecv[1] = jnp.zeros(hrecv.shape[1:], f32)

    arrived = jnp.concatenate([hrecv[0], hrecv[1]], 1)
    spread = jnp.concatenate([jnp.where(lane_group == r, arrived, 0.0) for r in range(groups)], 0)
    hi, lo = split(spread)
    xcat[:, 2 * points : 2 * points + 256] = hi
    xcat[:, 2 * points + 256 : 2 * points + 512] = lo

    entry = iota((256, points), 0)
    local_ids = iota((points, points), 0)
    halo_ids = points + jnp.where(entry >= 128, halo, 0) + entry % halo
    for s in range(slots):
        who = nb[s : s + 1, :]
        local = one_hot(who == local_ids).astype(bf16)
        edge = one_hot(who == halo_ids).astype(bf16)
        chosen = jnp.dot(
            xcat[...], jnp.concatenate([local, local, edge, edge], 0), preferred_element_type=f32
        ).reshape(dirs, PITCH, points)
        term = wgt[:, s : s + 1, :] * chosen
        if s == 0:
            spat[...] = term
        else:
            spat[...] += term

    for j in range(dirs):
        e = full(own + j)
        total = jnp.sum(wgt[j], axis=0, keepdims=True)
        turned = -jnp.abs(bend(j)) * e
        if j > 0:
            turned = turned + jnp.maximum(bend(j - 1), 0.0) * full(own + j - 1)
        if j < dirs - 1:
            turned = turned - jnp.minimum(bend(j + 1), 0.0) * full(own + j + 1)
        acc[own + j] += (e + speed_r[...] * (spat[j] - total * e) + turn_r[...] * turned)[0:freqs]

    for i, c in enumerate(order):
        chunk_copy(c).wait_recv()
        for a in range(CHUNK):
            w = chunk_slot(c) + a
            e32[w] = rbuf[c, a * freqs : (a + 1) * freqs, :]
            keep_split(w)
        if c == 0:
            acc[own + dirs - 1] -= turn_r[0:freqs] * (jnp.minimum(bend(dirs), 0.0) * e32[own + dirs])
        if c == CHUNKS:
            acc[own] += turn_r[0:freqs] * (jnp.maximum(bend(-1), 0.0) * e32[own - 1])
        if c < CHUNKS:
            quadruplets([chunk_slot(c) - REACH + a for a in range(CHUNK)])
        else:
            quadruplets([chunk_slot(c) + REACH + a for a in range(CHUNK)])
        done = CHUNK * (c % CHUNKS + 1)
        if i == 1:
            out[2 * REACH - done : dirs - 2 * REACH + done] = acc[own + 2 * REACH - done : own + dirs - 2 * REACH + done]
        elif i > 1:
            at = dirs - 2 * REACH + done - CHUNK if c < CHUNKS else 2 * REACH - done
            out[at : at + CHUNK] = acc[own + at : own + at + CHUNK]

    for k in order:
        chunk_copy(k).wait_send()

    @pl.when(t > 0)
    def _():
        halo_copy(1, t).wait_send()

    @pl.when(t < tiles - 1)
    def _():
        halo_copy(0, t).wait_send()


def body(tiles, spectrum, depths, refraction, edge_geometry, neighbours, send_rows, coupling, quad_table):
    dirs, freqs, points = spectrum.shape
    halo = send_rows.shape[0] // 2
    slots = neighbours.shape[0]
    ndir = 2 * dirs
    window = dirs + 4 * REACH
    lanes = (ndir * freqs + 127) // 128 * 128 + 128
    scratch = [
        pltpu.VMEM((window, freqs, points), f32),
        pltpu.VMEM((1, points), f32),
        pltpu.VMEM(refraction.shape, f32),
        pltpu.VMEM(edge_geometry.shape, f32),
        pltpu.VMEM(neighbours.shape, i32),
        pltpu.VMEM((1, 2 * halo), i32),
        pltpu.VMEM((1, freqs), f32),
        pltpu.VMEM(quad_table.shape, i32),
        pltpu.VMEM((window, PITCH_K, points), bf16),
        pltpu.VMEM((window, PITCH_K, points), bf16),
        pltpu.VMEM((window, freqs, points), f32),
        pltpu.VMEM((2 * CHUNKS, CHUNK * freqs, points), f32),
        pltpu.VMEM((2 * CHUNKS, CHUNK * freqs, points), f32),
        pltpu.VMEM((2, GROUP * PITCH, 128), f32),
        pltpu.VMEM((2, GROUP * PITCH, 128), f32),
        pltpu.VMEM((dirs * PITCH, 2 * points + 512), bf16),
        pltpu.VMEM((dirs, PITCH, points), f32),
        pltpu.VMEM((dirs, slots, points), f32),
        pltpu.VMEM((ndir, 8, 128), i32),
        pltpu.VMEM((ndir, PITCH, 128), i32),
        pltpu.VMEM((8, lanes), i32),
        pltpu.VMEM((lanes, 128), i32),
        pltpu.VMEM((8, 128), f32),
        pltpu.VMEM((8, 128), i32),
        pltpu.VMEM((PITCH, points), f32),
        pltpu.VMEM((PITCH, points), f32),
        pltpu.SemaphoreType.DMA((2 * CHUNKS + 8,)),
        pltpu.SemaphoreType.DMA((2 * CHUNKS,)),
        pltpu.SemaphoreType.DMA((2 * CHUNKS,)),
        pltpu.SemaphoreType.DMA((2,)),
        pltpu.SemaphoreType.DMA((2,)),
    ]
    return pl.pallas_call(
        functools.partial(kernel, dirs, freqs, points, halo, slots, tiles),
        out_shape=pltpu.VMEM(spectrum.shape, f32),
        in_specs=[pl.BlockSpec(memory_space=pl.ANY)] * 8,
        out_specs=pl.BlockSpec(memory_space=pltpu.VMEM),
        scratch_shapes=scratch,
        compiler_params=pltpu.CompilerParams(
            collective_id=0, has_side_effects=True, vmem_limit_bytes=VMEM
        ),
    )(
        spectrum,
        depths.reshape(1, points),
        refraction,
        edge_geometry,
        neighbours,
        send_rows.reshape(1, 2 * halo),
        coupling.reshape(1, freqs),
        quad_table,
    )


def solution(mesh):
    in_specs = (
        P("dir", None, "tile"),
        P("tile"),
        P(None, "tile"),
        P(None, None, "tile"),
        P(None, "tile"),
        P("tile"),
        P(),
        P(),
    )
    out_specs = P("dir", None, "tile")
    return jax.shard_map(
        functools.partial(body, mesh.shape["tile"]),
        mesh=mesh, in_specs=in_specs, out_specs=out_specs, check_vma=False,
    )
```
